256 devices in a mesh: seq: 64 (over x, y, z_lo, core), head: 4 (over z_hi).
Axes of the slice: x: 4, y: 4, z: 8 (z_hi: 4, z_lo: 2; z = z_hi * 2 + z_lo), core: 2. Of those that a mesh axis runs over, the one named last changes fastest.
Arguments:
- queries: bfloat16 [32768, 1408], P('seq', 'head'), may hold values from -8 to 8
- keys: bfloat16 [32768, 1408], P('seq', 'head'), may hold values from -8 to 8
- values: bfloat16 [32768, 1408], P('seq', 'head'), may hold values from -6 to 6
- lengths: int32 [16], replicated, may hold values from 1 to 4096, 32768 in all
- out_weight: bfloat16 [1408, 1408], P('head'), may hold values from -0.15625 to 0.15625
Outputs:
- projected: bfloat16 [32768, 1408], P('seq', 'head')
The draws below stay inside these ranges and needn't reach their ends.
Inputs may be any that keep to these rules, and one draw needn't show every extreme that they name: The lengths sum to 32768, each is 1 or more, and the largest is exactly 4096.
All inputs are finite; a program needn't handle non-finite values.
Results may differ from the reference program's by a relative error of at most 0.017.
Values may be sent and summed in bfloat16 or wider, within the bound.
A program may use at most 64 MiB of HBM per device.

```python
import math
import jax
import jax.numpy as jnp
import numpy as np
from jax import lax

D = 1408
HEADS = 16
HEAD_DIM = 88
TOK_DEV = 512
TOKENS = 32768
MOST = 4096
VIDEOS = 16


def draw_queries(key, part):
    key = jax.random.fold_in(key, 1)
    return jnp.clip(jax.random.normal(key, (TOKENS, D), jnp.float32), -6.0, 6.0).astype(jnp.bfloat16)


def draw_keys(key, part):
    key = jax.random.fold_in(key, 2)
    return jnp.clip(jax.random.normal(key, (TOKENS, D), jnp.float32), -6.0, 6.0).astype(jnp.bfloat16)


def steps_of(own_key, shape, pieces, least, high):
    level, own = 1.0, jax.random.fold_in(own_key, 6)
    for axis_at, shards_of in pieces:
        heights = jnp.exp(jax.random.uniform(jax.random.fold_in(own, axis_at), (shards_of,), jnp.float32, least / len(pieces), high / len(pieces)))
        level = level * jnp.repeat(heights, shape[axis_at] // shards_of).reshape([-1 if axis == axis_at else 1 for axis in range(len(shape))])
    return level


def split_up(count, total, bound, lean):
    loads = [(1 << 20) // math.isqrt(standing ** lean) + 1 for standing in range(2, count + 1)]
    surplus, counts = total - bound - (count - 1), [1] * (count - 1)
    while surplus > 0:
        movable = [i for i in range(count - 1) if counts[i] < bound]
        mass, remaining = sum([loads[i] for i in movable]), surplus
        for i in movable:
            addition = min(bound - counts[i], max(1, remaining * loads[i] // mass), surplus)
            counts[i] = counts[i] + addition
            surplus = surplus - addition
    return np.array([bound] + counts)


def ragged_sizes(key, number_of, total, most, lean):
    if number_of == 2:
        one = jax.random.randint(key, (), max(1, total - most), min(most, total - 1) + 1)
        return jnp.stack([one, total - one])
    sizes = jnp.asarray(split_up(number_of, total, most, lean), jnp.int32)
    twos = (number_of - 1) // 2
    donor, taker = sizes[1:1 + 2 * twos:2], sizes[2:2 + 2 * twos:2]
    slack = jnp.minimum(donor - 1, most - taker)
    moved = jax.random.randint(jax.random.fold_in(key, 1), (twos,), 0, 1 << 20) % (slack + 1)
    sizes = sizes.at[1:1 + 2 * twos:2].set(donor - moved).at[2:2 + 2 * twos:2].set(taker + moved)
    return sizes[jax.random.permutation(jax.random.fold_in(key, 2), number_of)]


def gaussian(key, shape, deviation, bound, cuts=(), kind=jnp.bfloat16):
    values = jax.random.normal(key, shape, jnp.float32) * deviation
    if len(cuts) > 0:
        values = steps_of(key, shape, cuts, -0.22, 0.18) * values
    return jnp.clip(values, min=-bound, max=bound).astype(kind)


def setup_inputs(seed: int = 0) -> dict:
    key_list = jax.random.split(jax.random.key(seed), 6)
    queries = draw_queries(jax.random.fold_in(key_list[5], 71), 0)
    keys = draw_keys(jax.random.fold_in(key_list[5], 71), 0)
    values = gaussian(key_list[2], (TOKENS, D), 1.0, 6.0, ((0, 64), (1, 4)))
    lengths = ragged_sizes(key_list[3], VIDEOS, TOKENS, MOST, 2).astype(jnp.int32)
    out_weight = gaussian(key_list[4], (D, D), D ** -0.5, 0.15625, ((0, 4),))
    return dict(queries=queries, keys=keys, values=values, lengths=lengths, out_weight=out_weight)


def reference(queries, keys, values, lengths, out_weight):
    tokens = queries.shape[0]
    ends = jnp.cumsum(lengths).astype(jnp.int32)
    positions = jnp.arange(tokens, dtype=jnp.int32)
    video = jnp.sum((ends[None, :] <= positions[:, None]).astype(jnp.int32), axis=1).astype(jnp.int32)
    keys_pad = jnp.pad(keys, ((MOST, MOST), (0, 0)))
    values_pad = jnp.pad(values, ((MOST, MOST), (0, 0)))
    video_pad = jnp.pad(video, (MOST, MOST), constant_values=-1).astype(jnp.int32)
    block = TOK_DEV
    window = block + 2 * MOST
    scale = 1.0 / (HEAD_DIM ** 0.5)

    def one_block(index):
        start = (index * block).astype(jnp.int32)
        query_rows = lax.dynamic_slice_in_dim(queries, start, block, 0).reshape(block, HEADS, HEAD_DIM).astype(jnp.float32)
        key_rows = lax.dynamic_slice_in_dim(keys_pad, start, window, 0).reshape(window, HEADS, HEAD_DIM).astype(jnp.float32)
        value_rows = lax.dynamic_slice_in_dim(values_pad, start, window, 0).reshape(window, HEADS, HEAD_DIM).astype(jnp.float32)
        video_q = lax.dynamic_slice_in_dim(video, start, block, 0)
        video_k = lax.dynamic_slice_in_dim(video_pad, start, window, 0)
        scores = jnp.einsum("qhd,khd->hqk", query_rows, key_rows) * scale
        kept = (video_q[:, None] == video_k[None, :])[None]
        scores = jnp.where(kept, scores, -1e30)
        top = jnp.max(scores, axis=-1, keepdims=True)
        weights = jnp.where(kept, jnp.exp(scores - top), 0.0)
        total = jnp.sum(weights, axis=-1)
        rounded = lax.optimization_barrier(weights.astype(jnp.bfloat16)).astype(jnp.float32)
        summed = jnp.einsum("hqk,khd->qhd", rounded, value_rows)
        attended = summed / jnp.transpose(total)[:, :, None]
        return attended.reshape(block, HEADS * HEAD_DIM).astype(jnp.bfloat16)

    attended = lax.map(one_block, jnp.arange(tokens // block, dtype=jnp.int32)).reshape(tokens, HEADS * HEAD_DIM)
    return jnp.dot(attended, out_weight, preferred_element_type=jnp.float32).astype(jnp.bfloat16)
```

```python
import functools

import jax
import jax.numpy as jnp
from jax import lax
from jax.experimental import pallas as pl
from jax.experimental.pallas import tpu as pltpu
from jax.sharding import PartitionSpec as P

HEAD_DIM = 88
PAD = 96
TOK = 512
QUAD = 4
TILE = 256
SLOTS = 20
EXPONENT = 1.4426950408889634 / HEAD_DIM**0.5
CODE = 1536.0
MESH = pl.DeviceIdType.MESH
F32 = jnp.float32
BF16 = jnp.bfloat16

S_KV, S_Q, S_NEAR, S_FAR, S_W, S_OWN, S_PAIR, S_PART, S_END = 0, 3, 6, 14, 22, 26, 32, 40, 42
R_KV, R_Q, R_W, R_OWN, R_PAIR, R_PART, R_END = 0, 20, 24, 28, 36, 44, 46


def video_code(lengths_ref, first_token, rows, offset):
    shape = (rows, TOK)
    pos = first_token + lax.broadcasted_iota(jnp.int32, shape, 1)
    row = lax.broadcasted_iota(jnp.int32, shape, 0) - offset
    video = jnp.zeros(shape, jnp.int32)
    end = 0
    for i in range(16):
        end = end + lengths_ref[i]
        video = video + jnp.where(pos >= end, 1, 0)
    both = row & video
    parity = (both ^ (both >> 1) ^ (both >> 2) ^ (video >> 3)) & 1
    return (1 - 2 * parity).astype(F32)


def kernel(
    lengths_ref, q_ref, k_ref, v_ref, w_ref, out_ref,
    kvs, qs, win, qw, kp, vp, qn, top, acc, wp, wr, ob, ao, ap, part, part_in,
    send, recv,
):
    seq, h = lax.axis_index("seq"), lax.axis_index("head")
    quads = lax.axis_size("seq") // QUAD
    g, j = seq // QUAD, seq % QUAD
    z, c = j // 2, j % 2
    left = ((g + quads - 1) % quads) * QUAD + j
    right = ((g + 1) % quads) * QUAD + j
    p1 = h + 1 - 2 * (h % 2)
    p2 = 3 - h

    def member(o):
        return 2 * ((z + o // 2) % 2) + (c + o % 2) % 2

    def copy(src, dst, s, r, seq_to, head_to):
        return pltpu.make_async_remote_copy(
            src_ref=src, dst_ref=dst, send_sem=send.at[s], recv_sem=recv.at[r],
            device_id=(seq_to, head_to), device_id_type=MESH,
        )

    barrier = pltpu.get_barrier_semaphore()

    def greet(seq_to, head_to):
        pl.semaphore_signal(barrier, inc=1, device_id=(seq_to, head_to), device_id_type=MESH)

    greet(left, h)
    greet(right, h)
    for o in range(QUAD):
        if o > 0:
            greet(g * QUAD + member(o), h)
        greet(g * QUAD + member(o), p1)
        greet(g * QUAD + member(o), p2)
    pl.semaphore_wait(barrier, 13)

    def one_hot(rows, shift):
        r = lax.broadcasted_iota(jnp.int32, (rows, QUAD * HEAD_DIM), 0) - shift
        col = lax.broadcasted_iota(jnp.int32, (rows, QUAD * HEAD_DIM), 1)
        return r, col

    def pick(hot, x):
        return lax.dot_general(hot, x, (((1,), (1,)), ((), ())), preferred_element_type=F32)

    def head_kv(i):
        r, col = one_hot(2 * HEAD_DIM, 0)
        of_k = jnp.where((r < HEAD_DIM) & (col == r + HEAD_DIM * i), 1.0, 0.0).astype(BF16)
        of_v = jnp.where((r >= HEAD_DIM) & (col == r + HEAD_DIM * (i - 1)), 1.0, 0.0).astype(BF16)
        return (pick(of_k, k_ref[...]) + pick(of_v, v_ref[...])).astype(BF16)

    own_code = video_code(lengths_ref, seq * TOK, PAD, HEAD_DIM)
    row96 = lax.broadcasted_iota(jnp.int32, (PAD, TOK), 0)

    def head_q(i):
        r, col = one_hot(PAD, 0)
        of_q = jnp.where((r < HEAD_DIM) & (col == r + HEAD_DIM * i), 1.0, 0.0).astype(BF16)
        return jnp.where(row96 < HEAD_DIM, pick(of_q, q_ref[...]), own_code).astype(BF16)

    def near(blk):
        for to, slot, way in ((right, 4, 0), (left, 12, 1)):
            copy(win.at[8 + blk], win.at[slot + blk], S_NEAR + 2 * blk + way, R_KV + slot + blk, to, h).start()

    def far(blk):
        for to, src, slot, way in ((right, 4, 0, 0), (left, 12, 16, 1)):
            copy(win.at[src + blk], win.at[slot + blk], S_FAR + 2 * blk + way, R_KV + slot + blk, to, h).start()

    win[8 + j] = head_kv(j)
    near(j)
    for o in (2, 3, 1):
        i = member(o)
        kvs[o - 1] = head_kv(i)
        copy(kvs.at[o - 1], win.at[8 + j], S_KV + o - 1, R_KV + 8 + j, g * QUAD + i, h).start()
    for o in (2, 3, 1):
        i = member(o)
        qs[o - 1] = head_q(i)
        copy(qs.at[o - 1], qw.at[j], S_Q + o - 1, R_Q + j, g * QUAD + i, h).start()
    qw[j] = head_q(j)

    r = lax.broadcasted_iota(jnp.int32, (QUAD * PAD, QUAD * HEAD_DIM), 0)
    col = lax.broadcasted_iota(jnp.int32, (QUAD * PAD, QUAD * HEAD_DIM), 1)
    spread = jnp.where((r % PAD >= PAD - HEAD_DIM) & (col == HEAD_DIM * (r // PAD) + r % PAD - (PAD - HEAD_DIM)), 1.0, 0.0)
    rows = jnp.dot(spread.astype(BF16), w_ref[...], preferred_element_type=F32)
    cols = QUAD * HEAD_DIM
    for b in range(4):
        wp[b] = rows[:, cols * b : cols * (b + 1)].astype(BF16)
    for half, pair, beyond in ((0, p1, 3 - p1), (1, p2, p2 + 1 - 2 * (p2 % 2))):
        for n, block in ((0, pair), (1, beyond)):
            copy(wp.at[block], wr.at[half, n], S_W + 2 * half + n, R_W + 2 * half + n, seq, pair).start()

    row16 = lax.broadcasted_iota(jnp.int32, (16, TOK), 0)

    def arrived(slot):
        copy(win.at[slot], win.at[slot], S_KV, R_KV + slot, seq, h).wait_recv()

    def augment(slot):
        blocks = quads * QUAD
        first = ((g * QUAD + slot - 8 + blocks) % blocks) * TOK
        code = (CODE * video_code(lengths_ref, first, 16, 8)).astype(BF16)
        middle = win[slot, 80:96, :]
        kp[slot, 0:80, :] = win[slot, 0:80, :]
        kp[slot, 80:96, :] = jnp.where(row16 < 8, middle, code)
        vp[slot, 0:16, :] = jnp.where(row16 < 8, jnp.ones_like(middle), middle)
        vp[slot, 16:96, :] = win[slot, 96:176, :]

    augment(8 + j)
    for o in range(1, QUAD):
        blk = member(o)
        arrived(8 + blk)
        near(blk)
        augment(8 + blk)
    for o in range(QUAD):
        blk = member(o)
        if o > 0:
            copy(qw.at[blk], qw.at[blk], S_Q, R_Q + blk, seq, h).wait_recv()
        qn[pl.ds(pl.multiple_of(blk * TOK, TOK), TOK), :] = qw[blk].T
    top[...] = jnp.full(top.shape, -1e30, F32)
    acc[...] = jnp.zeros(acc.shape, F32)

    def attend(at, slots):
        q = qn[at, :]
        scores = [jnp.dot(q, kp[s], preferred_element_type=F32) for s in slots]
        before = top[at, :]
        newest = before
        for s in scores:
            newest = jnp.maximum(newest, jnp.max(s, axis=1, keepdims=True))
        total = acc[at, :] * jnp.exp2((before - newest) * EXPONENT)
        for s, slot in zip(scores, slots):
            weights = jnp.exp2((s - newest) * EXPONENT).astype(BF16)
            total = total + lax.dot_general(
                weights, vp[slot], (((1,), (1,)), ((), ())), preferred_element_type=F32
            )
        return newest, total

    def rows_at(t):
        return pl.ds(pl.multiple_of(t * TILE, TILE), TILE)

    def own_step(o, carry):
        blk = member(o)
        for first in (4, 12):
            arrived(first + blk)
        far(blk)
        for first in (4, 12):
            augment(first + blk)

        def tile(n, carry):
            at = rows_at(2 * o + n)
            newest, total = attend(at, [8, 9, 10, 11])
            top[at, :] = newest
            acc[at, :] = total
            return carry

        return lax.fori_loop(0, 2, tile, carry)

    lax.fori_loop(0, QUAD, own_step, 0)

    def near_step(t, carry):
        at = rows_at(t)
        for slots in ([4, 5, 6, 7], [12, 13, 14, 15]):
            newest, total = attend(at, slots)
            top[at, :] = newest
            acc[at, :] = total
        return carry

    lax.fori_loop(0, 2 * QUAD, near_step, 0)

    def far_in(o, carry):
        blk = member(o)
        for first in (0, 16):
            arrived(first + blk)
            augment(first + blk)
        return carry

    lax.fori_loop(0, QUAD, far_in, 0)

    for half, pair in ((0, p1), (1, p2)):

        def far_step(n, carry):
            o = 3 - n
            b = member(o)
            at = rows_at(2 * b + half)
            newest, total = attend(at, [b + i + 12 * ((b + i) // 4) for i in range(5)])
            done = (total / total[:, 0:1]).T.astype(BF16)
            ob[half, b] = done
            to = g * QUAD + b

            @pl.when(o > 0)
            def _():
                copy(ob.at[half, b], ao.at[half, j], S_OWN + 3 * half + o - 1, R_OWN + 4 * half + j, to, h).start()

            copy(ob.at[half, b], ap.at[half, j], S_PAIR + 4 * half + o, R_PAIR + 4 * half + j, to, pair).start()
            return carry

        lax.fori_loop(0, QUAD, far_step, 0)
        ao[half, j] = ob[half, j]

    for n in range(4):
        copy(wr.at[n // 2, n % 2], wr.at[n // 2, n % 2], S_W, R_W + n, seq, h).wait_recv()
    sums = []
    for half, beyond in ((0, p2), (1, p1)):
        for o in range(QUAD):
            blk = member(o)
            if o > 0:
                copy(ao.at[half, blk], ao.at[half, blk], S_OWN, R_OWN + 4 * half + blk, seq, h).wait_recv()
            copy(ap.at[half, blk], ap.at[half, blk], S_PAIR, R_PAIR + 4 * half + blk, seq, h).wait_recv()
        mine = ao[half].reshape(QUAD * PAD, TILE).T
        other = ap[half].reshape(QUAD * PAD, TILE).T
        part[half] = (
            jnp.dot(mine, wp[beyond], preferred_element_type=F32)
            + jnp.dot(other, wr[half, 1], preferred_element_type=F32)
        ).astype(BF16)
        copy(part.at[half], part_in.at[half], S_PART + half, R_PART + half, seq, beyond).start()
        sums.append(
            jnp.dot(mine, wp[h], preferred_element_type=F32)
            + jnp.dot(other, wr[half, 0], preferred_element_type=F32)
        )
    for half in range(2):
        copy(part_in.at[half], part_in.at[half], S_PART, R_PART + half, seq, h).wait_recv()
        out_ref[half * TILE : (half + 1) * TILE, :] = (sums[half] + part_in[half].astype(F32)).astype(BF16)

    for o in range(3):
        copy(kvs.at[0], kvs.at[0], S_KV + o, R_KV, seq, h).wait_send()
        copy(qs.at[0], qs.at[0], S_Q + o, R_Q, seq, h).wait_send()
    for n in range(16):
        copy(win.at[0], win.at[0], S_NEAR + n, R_KV, seq, h).wait_send()
    for n in range(4):
        copy(wp.at[0], wp.at[0], S_W + n, R_W, seq, h).wait_send()
    for n in range(6):
        copy(ob.at[0, 0], ob.at[0, 0], S_OWN + n, R_OWN, seq, h).wait_send()
    for n in range(8):
        copy(ob.at[0, 0], ob.at[0, 0], S_PAIR + n, R_PAIR, seq, h).wait_send()
    for n in range(2):
        copy(part.at[0], part.at[0], S_PART + n, R_PART, seq, h).wait_send()


def body(queries, keys, values, lengths, out_weight):
    cols = QUAD * HEAD_DIM
    vmem = pl.BlockSpec(memory_space=pltpu.VMEM)
    return pl.pallas_call(
        kernel,
        out_shape=jax.ShapeDtypeStruct((TOK, cols), BF16),
        in_specs=[pl.BlockSpec(memory_space=pltpu.SMEM)] + [vmem] * 4,
        out_specs=vmem,
        scratch_shapes=[
            pltpu.VMEM((3, 2 * HEAD_DIM, TOK), BF16),
            pltpu.VMEM((3, PAD, TOK), BF16),
            pltpu.VMEM((SLOTS, 2 * HEAD_DIM, TOK), BF16),
            pltpu.VMEM((QUAD, PAD, TOK), BF16),
            pltpu.VMEM((SLOTS, PAD, TOK), BF16),
            pltpu.VMEM((SLOTS, PAD, TOK), BF16),
            pltpu.VMEM((QUAD * TOK, PAD), BF16),
            pltpu.VMEM((QUAD * TOK, 1), F32),
            pltpu.VMEM((QUAD * TOK, PAD), F32),
            pltpu.VMEM((4, QUAD * PAD, cols), BF16),
            pltpu.VMEM((2, 2, QUAD * PAD, cols), BF16),
            pltpu.VMEM((2, QUAD, PAD, TILE), BF16),
            pltpu.VMEM((2, QUAD, PAD, TILE), BF16),
            pltpu.VMEM((2, QUAD, PAD, TILE), BF16),
            pltpu.VMEM((2, TILE, cols), BF16),
            pltpu.VMEM((2, TILE, cols), BF16),
            pltpu.SemaphoreType.DMA((S_END,)),
            pltpu.SemaphoreType.DMA((R_END,)),
        ],
        compiler_params=pltpu.CompilerParams(
            collective_id=0, has_side_effects=True, vmem_limit_bytes=56 << 20
        ),
    )(lengths, queries, keys, values, out_weight)


def solution(mesh):
    in_specs = (P("seq", "head"), P("seq", "head"), P("seq", "head"), P(), P("head", None))
    out_specs = P("seq", "head")
    return jax.shard_map(body, mesh=mesh, in_specs=in_specs, out_specs=out_specs, check_vma=False)
```

```python
import functools

import jax
import jax.numpy as jnp
from jax import lax
from jax.experimental import pallas as pl
from jax.experimental.pallas import tpu as pltpu
from jax.sharding import PartitionSpec as P

HEAD_DIM = 88
PAD = 96
TOK = 512
QUAD = 4
TILE = 256
SLOTS = 20
EXPONENT = 1.4426950408889634 / HEAD_DIM**0.5
CODE = 1536.0
MESH = pl.DeviceIdType.MESH
F32 = jnp.float32
BF16 = jnp.bfloat16

S_KV, S_Q, S_NEAR, S_FAR, S_W, S_WQ, S_OWN, S_PAIR, S_PART, S_END = 0, 4, 8, 16, 24, 25, 29, 33, 41, 43
R_KV, R_Q, R_W, R_OWN, R_PAIR, R_PART, R_END = 0, 20, 24, 28, 32, 40, 42


def video_code(lengths_ref, first_token, rows, offset):
    shape = (rows, TOK)
    pos = first_token + lax.broadcasted_iota(jnp.int32, shape, 1)
    row = lax.broadcasted_iota(jnp.int32, shape, 0) - offset
    video = jnp.zeros(shape, jnp.int32)
    end = 0
    for i in range(16):
        end = end + lengths_ref[i]
        video = video + jnp.where(pos >= end, 1, 0)
    both = row & video
    parity = (both ^ (both >> 1) ^ (both >> 2) ^ (video >> 3)) & 1
    return (1 - 2 * parity).astype(F32)


def kernel(
    lengths_ref, q_ref, k_ref, v_ref, w_ref, out_ref,
    kvs, qs, win, qw, kp, vp, qn, top, acc, wp, wr, ob, ao, ap, part, part_in,
    send, recv,
):
    seq, h = lax.axis_index("seq"), lax.axis_index("head")
    quads = lax.axis_size("seq") // QUAD
    g, j = seq // QUAD, seq % QUAD
    z, c = j // 2, j % 2
    left = ((g + quads - 1) % quads) * QUAD + j
    right = ((g + 1) % quads) * QUAD + j
    p1 = h + 1 - 2 * (h % 2)
    p2 = 3 - h

    def member(o):
        return 2 * ((z + o // 2) % 2) + (c + o % 2) % 2

    def copy(src, dst, s, r, seq_to, head_to):
        return pltpu.make_async_remote_copy(
            src_ref=src, dst_ref=dst, send_sem=send.at[s], recv_sem=recv.at[r],
            device_id=(seq_to, head_to), device_id_type=MESH,
        )

    barrier = pltpu.get_barrier_semaphore()

    def greet(seq_to, head_to):
        pl.semaphore_signal(barrier, inc=1, device_id=(seq_to, head_to), device_id_type=MESH)

    greet(left, h)
    greet(right, h)
    for o in range(QUAD):
        if o > 0:
            greet(g * QUAD + member(o), h)
        greet(g * QUAD + member(o), p1)
        greet(g * QUAD + member(o), p2)

    for i in range(QUAD):
        rows = slice(HEAD_DIM * i, HEAD_DIM * (i + 1))
        kvs[i] = jnp.concatenate([k_ref[rows, :], v_ref[rows, :]], axis=0)
    own_code = video_code(lengths_ref, seq * TOK, 8, 0).astype(BF16)
    for i in range(QUAD):
        rows = slice(HEAD_DIM * i, HEAD_DIM * (i + 1))
        qs[i] = jnp.concatenate([q_ref[rows, :], own_code], axis=0)
    pl.semaphore_wait(barrier, 13)

    def near(src, blk):
        for to, slot, way in ((right, 4, 0), (left, 12, 1)):
            copy(src, win.at[slot + blk], S_NEAR + 2 * blk + way, R_KV + slot + blk, to, h).start()

    near(kvs.at[j], j)
    for o in (2, 3, 1):
        i = member(o)
        copy(kvs.at[i], win.at[8 + j], S_KV + o, R_KV + 8 + j, g * QUAD + i, h).start()
    for o in (2, 3, 1):
        i = member(o)
        copy(qs.at[i], qw.at[j], S_Q + o, R_Q + j, g * QUAD + i, h).start()
    win[8 + j] = kvs[j]
    qw[j] = qs[j]

    cols = QUAD * HEAD_DIM
    r = lax.broadcasted_iota(jnp.int32, (cols, QUAD * PAD), 0)
    col = lax.broadcasted_iota(jnp.int32, (cols, QUAD * PAD), 1)
    from_row = HEAD_DIM * (col // PAD) + col % PAD - (PAD - HEAD_DIM)
    spread = jnp.where((col % PAD >= PAD - HEAD_DIM) & (r == from_row), 1.0, 0.0).astype(BF16)
    for b in range(4):
        wp[b] = lax.dot_general(
            w_ref[:, cols * b : cols * (b + 1)], spread, (((0,), (0,)), ((), ())), preferred_element_type=F32
        ).astype(BF16)
    pair = jnp.where(j < 2, p1, p2)
    other = jnp.where(j < 2, 3 - p1, p2 + 1 - 2 * (p2 % 2))
    copy(wp.at[jnp.where(j % 2 == 0, pair, other)], wr.at[j], S_W, R_W + j, seq, pair).start()

    row16 = lax.broadcasted_iota(jnp.int32, (16, TOK), 0)

    def arrived(slot):
        copy(win.at[slot], win.at[slot], S_KV, R_KV + slot, seq, h).wait_recv()

    def augment(slot):
        blocks = quads * QUAD
        first = ((g * QUAD + slot - 8 + blocks) % blocks) * TOK
        code = (CODE * video_code(lengths_ref, first, 16, 8)).astype(BF16)
        middle = win[slot, 80:96, :]
        kp[slot, 0:80, :] = win[slot, 0:80, :]
        kp[slot, 80:96, :] = jnp.where(row16 < 8, middle, code)
        vp[slot, 0:16, :] = jnp.where(row16 < 8, jnp.ones_like(middle), middle)
        vp[slot, 16:96, :] = win[slot, 96:176, :]

    augment(8 + j)
    for o in range(1, QUAD):
        blk = member(o)
        arrived(8 + blk)
        near(win.at[8 + blk], blk)
        augment(8 + blk)
    for o in range(QUAD):
        blk = member(o)
        if o > 0:
            copy(qw.at[blk], qw.at[blk], S_Q, R_Q + blk, seq, h).wait_recv()
        qn[pl.ds(pl.multiple_of(blk * TOK, TOK), TOK), :] = qw[blk].T

    def attend(t, slots, opening=False):
        at = slice(t * TILE, (t + 1) * TILE)
        q = qn[at, :]
        scores = [jnp.dot(q, kp[s], preferred_element_type=F32) for s in slots]
        newest = jnp.max(scores[0], axis=1, keepdims=True)
        for s in scores[1:]:
            newest = jnp.maximum(newest, jnp.max(s, axis=1, keepdims=True))
        total = None
        if not opening:
            before = top[at, :]
            newest = jnp.maximum(before, newest)
            total = acc[at, :] * jnp.exp2((before - newest) * EXPONENT)
        for s, slot in zip(scores, slots):
            weights = jnp.exp2((s - newest) * EXPONENT).astype(BF16)
            term = lax.dot_general(weights, vp[slot], (((1,), (1,)), ((), ())), preferred_element_type=F32)
            total = term if total is None else total + term
        top[at, :] = newest
        acc[at, :] = total

    for t in range(2 * QUAD):
        attend(t, [8, 9, 10, 11], opening=True)

    copy(wr.at[j], wr.at[j], S_W, R_W + j, seq, h).wait_recv()
    for o in range(1, QUAD):
        copy(wr.at[j], wr.at[j], S_WQ + o, R_W + j, g * QUAD + member(o), h).start()

    for n in range(QUAD):
        for to, src, slot, blk, way in ((right, 4, 0, 3 - n, 0), (left, 12, 16, n, 1)):
            arrived(src + blk)
            copy(win.at[src + blk], win.at[slot + blk], S_FAR + 2 * blk + way, R_KV + slot + blk, to, h).start()
    for n in range(QUAD):
        augment(4 + n)
        augment(12 + n)
    for t in range(2 * QUAD):
        attend(t, [4, 5, 6, 7, 12, 13, 14, 15])

    def finish(b):
        for half, pair in ((0, p1), (1, p2)):
            at = slice((2 * b + half) * TILE, (2 * b + half + 1) * TILE)
            total = acc[at, :]
            ob[b, :, half * TILE : (half + 1) * TILE] = (total / total[:, 0:1]).T.astype(BF16)
        to = g * QUAD + b

        @pl.when(j != b)
        def _():
            copy(ob.at[b], ao.at[j], S_OWN + b, R_OWN + j, to, h).start()

        for half, pair in ((0, p1), (1, p2)):
            copy(
                ob.at[b, :, pl.ds(half * TILE, TILE)], ap.at[half, j],
                S_PAIR + 2 * b + half, R_PAIR + 4 * half + j, to, pair,
            ).start()

        @pl.when(j == b)
        def _():
            ao[j] = ob[b]

    def far_round(n, work):
        for slot in (3 - n, 16 + n):
            arrived(slot)
            augment(slot)
        for b, slots in work:
            for half in range(2):
                attend(2 * b + half, slots)

    far_round(0, [(b, [3, 16]) for b in range(4)])
    far_round(1, [(0, [2]), (1, [2, 17]), (2, [2, 17]), (3, [17])])
    far_round(2, [(1, [1]), (2, [18])])
    finish(1)
    finish(2)
    for b, slot in ((0, 1), (3, 18)):
        for half in range(2):
            attend(2 * b + half, [slot])
    far_round(3, [(0, [0]), (3, [19])])
    finish(0)
    finish(3)

    for o in range(1, QUAD):
        blk = member(o)
        copy(wr.at[blk], wr.at[blk], S_W, R_W + blk, seq, h).wait_recv()
    for o in range(1, QUAD):
        blk = member(o)
        copy(ao.at[blk], ao.at[blk], S_OWN, R_OWN + blk, seq, h).wait_recv()
    sums = []
    for half, beyond in ((0, p2), (1, p1)):
        for blk in range(QUAD):
            copy(ap.at[half, blk], ap.at[half, blk], S_PAIR, R_PAIR + 4 * half + blk, seq, h).wait_recv()
        mine = ao[:, :, half * TILE : (half + 1) * TILE].reshape(QUAD * PAD, TILE)
        theirs = ap[half].reshape(QUAD * PAD, TILE)
        part[half] = (
            jnp.dot(wp[beyond], mine, preferred_element_type=F32)
            + jnp.dot(wr[2 * half + 1], theirs, preferred_element_type=F32)
        ).astype(BF16)
        copy(part.at[half], part_in.at[half], S_PART + half, R_PART + half, seq, beyond).start()
        sums.append(
            jnp.dot(wp[h], mine, preferred_element_type=F32)
            + jnp.dot(wr[2 * half], theirs, preferred_element_type=F32)
        )
    for half in range(2):
        copy(part_in.at[half], part_in.at[half], S_PART, R_PART + half, seq, h).wait_recv()
        out_ref[:, half * TILE : (half + 1) * TILE] = (sums[half] + part_in[half].astype(F32)).astype(BF16)

    for o in range(1, QUAD):
        copy(kvs.at[0], kvs.at[0], S_KV + o, R_KV, seq, h).wait_send()
        copy(qs.at[0], qs.at[0], S_Q + o, R_Q, seq, h).wait_send()
        copy(wr.at[0], wr.at[0], S_WQ + o, R_W, seq, h).wait_send()
    for n in range(16):
        copy(win.at[0], win.at[0], S_NEAR + n, R_KV, seq, h).wait_send()
    copy(wp.at[0], wp.at[0], S_W, R_W, seq, h).wait_send()
    for b in range(QUAD):

        @pl.when(j != b)
        def _():
            copy(ob.at[0], ob.at[0], S_OWN + b, R_OWN, seq, h).wait_send()

    for n in range(8):
        copy(ap.at[0, 0], ap.at[0, 0], S_PAIR + n, R_PAIR, seq, h).wait_send()
    for n in range(2):
        copy(part.at[0], part.at[0], S_PART + n, R_PART, seq, h).wait_send()


def body(queries, keys, values, lengths, out_weight):
    cols = QUAD * HEAD_DIM
    vmem = pl.BlockSpec(memory_space=pltpu.VMEM)
    out = pl.pallas_call(
        kernel,
        out_shape=jax.ShapeDtypeStruct((cols, TOK), BF16),
        in_specs=[pl.BlockSpec(memory_space=pltpu.SMEM)] + [vmem] * 4,
        out_specs=vmem,
        scratch_shapes=[
            pltpu.VMEM((QUAD, 2 * HEAD_DIM, TOK), BF16),
            pltpu.VMEM((QUAD, PAD, TOK), BF16),
            pltpu.VMEM((SLOTS, 2 * HEAD_DIM, TOK), BF16),
            pltpu.VMEM((QUAD, PAD, TOK), BF16),
            pltpu.VMEM((SLOTS, PAD, TOK), BF16),
            pltpu.VMEM((SLOTS, PAD, TOK), BF16),
            pltpu.VMEM((QUAD * TOK, PAD), BF16),
            pltpu.VMEM((QUAD * TOK, 1), F32),
            pltpu.VMEM((QUAD * TOK, PAD), F32),
            pltpu.VMEM((4, cols, QUAD * PAD), BF16),
            pltpu.VMEM((4, cols, QUAD * PAD), BF16),
            pltpu.VMEM((QUAD, PAD, TOK), BF16),
            pltpu.VMEM((QUAD, PAD, TOK), BF16),
            pltpu.VMEM((2, QUAD, PAD, TILE), BF16),
            pltpu.VMEM((2, cols, TILE), BF16),
            pltpu.VMEM((2, cols, TILE), BF16),
            pltpu.SemaphoreType.DMA((S_END,)),
            pltpu.SemaphoreType.DMA((R_END,)),
        ],
        compiler_params=pltpu.CompilerParams(
            collective_id=0, has_side_effects=True, vmem_limit_bytes=56 << 20
        ),
    )(lengths, queries.T, keys.T, values.T, out_weight)
    return out.T


def solution(mesh):
    in_specs = (P("seq", "head"), P("seq", "head"), P("seq", "head"), P(), P("head", None))
    out_specs = P("seq", "head")
    return jax.shard_map(body, mesh=mesh, in_specs=in_specs, out_specs=out_specs, check_vma=False)
```

```python
import functools

import jax
import jax.numpy as jnp
from jax import lax
from jax.experimental import pallas as pl
from jax.experimental.pallas import tpu as pltpu
from jax.sharding import PartitionSpec as P

HEAD_DIM = 88
PAD = 96
TOK = 512
QUAD = 4
TILE = 256
SLOTS = 20
EXPONENT = 1.4426950408889634 / HEAD_DIM**0.5
CODE = 1536.0
MESH = pl.DeviceIdType.MESH
F32 = jnp.float32
BF16 = jnp.bfloat16

S_KV, S_Q, S_NEAR, S_FAR, S_W, S_WQ, S_OWN, S_PAIR, S_PART, S_END = 0, 4, 8, 16, 24, 25, 29, 33, 41, 43
R_KV, R_Q, R_W, R_OWN, R_PAIR, R_PART, R_END = 0, 20, 24, 28, 32, 40, 42


def video_code(lengths_ref, first_token, rows, offset):
    shape = (rows, TOK)
    pos = first_token + lax.broadcasted_iota(jnp.int32, shape, 1)
    row = lax.broadcasted_iota(jnp.int32, shape, 0) - offset
    video = jnp.zeros(shape, jnp.int32)
    end = 0
    for i in range(16):
        end = end + lengths_ref[i]
        video = video + jnp.where(pos >= end, 1, 0)
    both = row & video
    parity = (both ^ (both >> 1) ^ (both >> 2) ^ (video >> 3)) & 1
    return (1 - 2 * parity).astype(F32)


def kernel(
    lengths_ref, q_ref, k_ref, v_ref, w_ref, out_ref,
    kvs, qs, win, qw, kp, vp, qn, top, acc, wp, wr, ob, ao, ap, part, part_in,
    send, recv,
):
    seq, h = lax.axis_index("seq"), lax.axis_index("head")
    quads = lax.axis_size("seq") // QUAD
    g, j = seq // QUAD, seq % QUAD
    z, c = j // 2, j % 2
    left = ((g + quads - 1) % quads) * QUAD + j
    right = ((g + 1) % quads) * QUAD + j
    p1 = h + 1 - 2 * (h % 2)
    p2 = 3 - h

    def member(o):
        return 2 * ((z + o // 2) % 2) + (c + o % 2) % 2

    def copy(src, dst, s, r, seq_to, head_to):
        return pltpu.make_async_remote_copy(
            src_ref=src, dst_ref=dst, send_sem=send.at[s], recv_sem=recv.at[r],
            device_id=(seq_to, head_to), device_id_type=MESH,
        )

    barrier = pltpu.get_barrier_semaphore()

    def greet(seq_to, head_to):
        pl.semaphore_signal(barrier, inc=1, device_id=(seq_to, head_to), device_id_type=MESH)

    greet(left, h)
    greet(right, h)
    for o in range(QUAD):
        if o > 0:
            greet(g * QUAD + member(o), h)
        greet(g * QUAD + member(o), p1)
        greet(g * QUAD + member(o), p2)

    for i in range(QUAD):
        rows = slice(HEAD_DIM * i, HEAD_DIM * (i + 1))
        kvs[i] = jnp.concatenate([k_ref[rows, :], v_ref[rows, :]], axis=0)
    own_code = video_code(lengths_ref, seq * TOK, 8, 0).astype(BF16)
    for i in range(QUAD):
        rows = slice(HEAD_DIM * i, HEAD_DIM * (i + 1))
        qs[i] = jnp.concatenate([q_ref[rows, :], own_code], axis=0)
    pl.semaphore_wait(barrier, 13)

    def near(src, blk):
        for to, slot, way in ((right, 4, 0), (left, 12, 1)):
            copy(src, win.at[slot + blk], S_NEAR + 2 * blk + way, R_KV + slot + blk, to, h).start()

    near(kvs.at[j], j)
    for o in (2, 3, 1):
        i = member(o)
        copy(kvs.at[i], win.at[8 + j], S_KV + o, R_KV + 8 + j, g * QUAD + i, h).start()
    for o in (2, 3, 1):
        i = member(o)
        copy(qs.at[i], qw.at[j], S_Q + o, R_Q + j, g * QUAD + i, h).start()
    win[8 + j] = kvs[j]
    qw[j] = qs[j]

    cols = QUAD * HEAD_DIM
    r = lax.broadcasted_iota(jnp.int32, (cols, QUAD * PAD), 0)
    col = lax.broadcasted_iota(jnp.int32, (cols, QUAD * PAD), 1)
    from_row = HEAD_DIM * (col // PAD) + col % PAD - (PAD - HEAD_DIM)
    spread = jnp.where((col % PAD >= PAD - HEAD_DIM) & (r == from_row), 1.0, 0.0).astype(BF16)
    for b in range(4):
        wp[b] = lax.dot_general(
            w_ref[:, cols * b : cols * (b + 1)], spread, (((0,), (0,)), ((), ())), preferred_element_type=F32
        ).astype(BF16)
    to_pair = jnp.where(z == 1, (h + 1) % 4, (h + 3) % 4)
    pair_1 = to_pair + 1 - 2 * (to_pair % 2)
    beyond = jnp.where(pair_1 == h, 3 - to_pair, pair_1)
    piece = 2 * (1 - (h + z) % 2) + c
    copy(
        wp.at[jnp.where(c == 0, to_pair, beyond)], wr.at[piece], S_W, R_W + piece,
        g * QUAD + 2 * (1 - z) + c, to_pair,
    ).start()

    row16 = lax.broadcasted_iota(jnp.int32, (16, TOK), 0)

    def arrived(slot):
        copy(win.at[slot], win.at[slot], S_KV, R_KV + slot, seq, h).wait_recv()

    def augment(slot):
        blocks = quads * QUAD
        first = ((g * QUAD + slot - 8 + blocks) % blocks) * TOK
        code = (CODE * video_code(lengths_ref, first, 16, 8)).astype(BF16)
        middle = win[slot, 80:96, :]
        kp[slot, 0:80, :] = win[slot, 0:80, :]
        kp[slot, 80:96, :] = jnp.where(row16 < 8, middle, code)
        vp[slot, 0:16, :] = jnp.where(row16 < 8, jnp.ones_like(middle), middle)
        vp[slot, 16:96, :] = win[slot, 96:176, :]

    def queries_of(blk):
        qn[pl.ds(pl.multiple_of(blk * TOK, TOK), TOK), :] = qw[blk].T

    def attend(t, slots, opening=False):
        at = pl.ds(t * TILE if isinstance(t, int) else pl.multiple_of(t * TILE, TILE), TILE)
        q = qn[at, :]
        scores = [jnp.dot(q, kp[s], preferred_element_type=F32) for s in slots]
        newest = jnp.max(scores[0], axis=1, keepdims=True)
        for s in scores[1:]:
            newest = jnp.maximum(newest, jnp.max(s, axis=1, keepdims=True))
        total = None
        if not opening:
            before = top[at, :]
            newest = jnp.maximum(before, newest)
            total = acc[at, :] * jnp.exp2((before - newest) * EXPONENT)
        for s, slot in zip(scores, slots):
            weights = jnp.exp2((s - newest) * EXPONENT).astype(BF16)
            term = lax.dot_general(weights, vp[slot], (((1,), (1,)), ((), ())), preferred_element_type=F32)
            total = term if total is None else total + term
        top[at, :] = newest
        acc[at, :] = total

    def attend_block(blk, slots, opening=False):
        for half in range(2):
            attend(2 * blk + half, slots, opening)

    here, there = [j, member(1)], [member(2), member(3)]

    augment(8 + j)
    queries_of(j)
    arrived(8 + here[1])
    near(win.at[8 + here[1]], here[1])
    augment(8 + here[1])
    copy(qw.at[here[1]], qw.at[here[1]], S_Q, R_Q + here[1], seq, h).wait_recv()
    queries_of(here[1])
    for blk in here:
        attend_block(blk, [8 + i for i in here], opening=True)
    for blk in there:
        arrived(8 + blk)
        near(win.at[8 + blk], blk)
    for blk in there:
        augment(8 + blk)
    for blk in here:
        for first in (4, 12):
            arrived(first + blk)
            augment(first + blk)
    early = [first + i for first in (4, 12) for i in here]
    for blk in here:
        attend_block(blk, [8 + i for i in there] + early)
    for blk in there:
        copy(qw.at[blk], qw.at[blk], S_Q, R_Q + blk, seq, h).wait_recv()
        queries_of(blk)
    for blk in there:
        attend_block(blk, [8, 9, 10, 11] + early, opening=True)

    for blk in there:
        for first in (4, 12):
            arrived(first + blk)
    for n in range(QUAD):
        for to, src, slot, blk, way in ((right, 4, 0, 3 - n, 0), (left, 12, 16, n, 1)):
            copy(win.at[src + blk], win.at[slot + blk], S_FAR + 2 * blk + way, R_KV + slot + blk, to, h).start()
    copy(wr.at[piece], wr.at[piece], S_W, R_W + piece, seq, h).wait_recv()
    for o in range(1, QUAD):
        copy(wr.at[piece], wr.at[piece], S_WQ + o, R_W + piece, g * QUAD + member(o), h).start()
    for blk in there:
        for first in (4, 12):
            augment(first + blk)
    for blk in range(QUAD):
        attend_block(blk, [first + i for first in (4, 12) for i in there])

    def finish(b):
        for half, pair in ((0, p1), (1, p2)):
            at = slice((2 * b + half) * TILE, (2 * b + half + 1) * TILE)
            total = acc[at, :]
            ob[b, :, half * TILE : (half + 1) * TILE] = (total / total[:, 0:1]).T.astype(BF16)
        to = g * QUAD + b

        @pl.when(j != b)
        def _():
            copy(ob.at[b], ao.at[j], S_OWN + b, R_OWN + j, to, h).start()

        for half, pair in ((0, p1), (1, p2)):
            copy(
                ob.at[b, :, pl.ds(half * TILE, TILE)], ap.at[half, j],
                S_PAIR + 2 * b + half, R_PAIR + 4 * half + j, to, pair,
            ).start()

        @pl.when(j == b)
        def _():
            ao[j] = ob[b]

    def far_round(n, work):
        for slot in (3 - n, 16 + n):
            arrived(slot)
            augment(slot)
        for b, slots in work:
            attend_block(b, slots)

    far_round(0, [(b, [3, 16]) for b in range(4)])
    far_round(1, [(0, [2]), (1, [2, 17]), (2, [2, 17]), (3, [17])])
    far_round(2, [(1, [1]), (2, [18])])
    finish(1)
    finish(2)
    for b, slot in ((0, 1), (3, 18)):
        attend_block(b, [slot])
    far_round(3, [(0, [0]), (3, [19])])
    finish(0)
    finish(3)

    for o in range(1, QUAD):
        i = member(o)
        i = 2 * (1 - (h + i // 2) % 2) + i % 2
        copy(wr.at[i], wr.at[i], S_W, R_W + i, seq, h).wait_recv()
    for o in range(1, QUAD):
        blk = member(o)
        copy(ao.at[blk], ao.at[blk], S_OWN, R_OWN + blk, seq, h).wait_recv()
    sums = []
    for half, beyond in ((0, p2), (1, p1)):
        for blk in range(QUAD):
            copy(ap.at[half, blk], ap.at[half, blk], S_PAIR, R_PAIR + 4 * half + blk, seq, h).wait_recv()
        mine = ao[:, :, half * TILE : (half + 1) * TILE].reshape(QUAD * PAD, TILE)
        theirs = ap[half].reshape(QUAD * PAD, TILE)
        part[half] = (
            jnp.dot(wp[beyond], mine, preferred_element_type=F32)
            + jnp.dot(wr[2 * half + 1], theirs, preferred_element_type=F32)
        ).astype(BF16)
        copy(part.at[half], part_in.at[half], S_PART + half, R_PART + half, seq, beyond).start()
        sums.append(
            jnp.dot(wp[h], mine, preferred_element_type=F32)
            + jnp.dot(wr[2 * half], theirs, preferred_element_type=F32)
        )
    for half in range(2):
        copy(part_in.at[half], part_in.at[half], S_PART, R_PART + half, seq, h).wait_recv()
        out_ref[:, half * TILE : (half + 1) * TILE] = (sums[half] + part_in[half].astype(F32)).astype(BF16)

    for o in range(1, QUAD):
        copy(kvs.at[0], kvs.at[0], S_KV + o, R_KV, seq, h).wait_send()
        copy(qs.at[0], qs.at[0], S_Q + o, R_Q, seq, h).wait_send()
        copy(wr.at[0], wr.at[0], S_WQ + o, R_W, seq, h).wait_send()
    for n in range(16):
        copy(win.at[0], win.at[0], S_NEAR + n, R_KV, seq, h).wait_send()
    copy(wp.at[0], wp.at[0], S_W, R_W, seq, h).wait_send()
    for b in range(QUAD):

        @pl.when(j != b)
        def _():
            copy(ob.at[0], ob.at[0], S_OWN + b, R_OWN, seq, h).wait_send()

    for n in range(8):
        copy(ap.at[0, 0], ap.at[0, 0], S_PAIR + n, R_PAIR, seq, h).wait_send()
    for n in range(2):
        copy(part.at[0], part.at[0], S_PART + n, R_PART, seq, h).wait_send()


def body(queries, keys, values, lengths, out_weight):
    cols = QUAD * HEAD_DIM
    vmem = pl.BlockSpec(memory_space=pltpu.VMEM)
    out = pl.pallas_call(
        kernel,
        out_shape=jax.ShapeDtypeStruct((cols, TOK), BF16),
        in_specs=[pl.BlockSpec(memory_space=pltpu.SMEM)] + [vmem] * 4,
        out_specs=vmem,
        scratch_shapes=[
            pltpu.VMEM((QUAD, 2 * HEAD_DIM, TOK), BF16),
            pltpu.VMEM((QUAD, PAD, TOK), BF16),
            pltpu.VMEM((SLOTS, 2 * HEAD_DIM, TOK), BF16),
            pltpu.VMEM((QUAD, PAD, TOK), BF16),
            pltpu.VMEM((SLOTS, PAD, TOK), BF16),
            pltpu.VMEM((SLOTS, PAD, TOK), BF16),
            pltpu.VMEM((QUAD * TOK, PAD), BF16),
            pltpu.VMEM((QUAD * TOK, 1), F32),
            pltpu.VMEM((QUAD * TOK, PAD), F32),
            pltpu.VMEM((4, cols, QUAD * PAD), BF16),
            pltpu.VMEM((4, cols, QUAD * PAD), BF16),
            pltpu.VMEM((QUAD, PAD, TOK), BF16),
            pltpu.VMEM((QUAD, PAD, TOK), BF16),
            pltpu.VMEM((2, QUAD, PAD, TILE), BF16),
            pltpu.VMEM((2, cols, TILE), BF16),
            pltpu.VMEM((2, cols, TILE), BF16),
            pltpu.SemaphoreType.DMA((S_END,)),
            pltpu.SemaphoreType.DMA((R_END,)),
        ],
        compiler_params=pltpu.CompilerParams(
            collective_id=0, has_side_effects=True, vmem_limit_bytes=56 << 20
        ),
    )(lengths, queries.T, keys.T, values.T, out_weight)
    return out.T


def solution(mesh):
    in_specs = (P("seq", "head"), P("seq", "head"), P("seq", "head"), P(), P("head", None))
    out_specs = P("seq", "head")
    return jax.shard_map(body, mesh=mesh, in_specs=in_specs, out_specs=out_specs, check_vma=False)
```

```python
import functools

import jax
import jax.numpy as jnp
from jax import lax
from jax.experimental import pallas as pl
from jax.experimental.pallas import tpu as pltpu
from jax.sharding import PartitionSpec as P

HEAD_DIM = 88
PAD = 96
TOK = 512
QUAD = 4
TILE = 256
SLOTS = 20
EXPONENT = 1.4426950408889634 / HEAD_DIM**0.5
CODE = 1536.0
MESH = pl.DeviceIdType.MESH
F32 = jnp.float32
BF16 = jnp.bfloat16

S_KV, S_Q, S_NEAR, S_FAR, S_W, S_WQ, S_OWN, S_PAIR, S_PART, S_END = 0, 4, 8, 16, 24, 25, 29, 33, 41, 43
R_KV, R_Q, R_W, R_OWN, R_PAIR, R_PART, R_END = 0, 20, 24, 28, 32, 40, 42


def video_code(lengths_ref, first_token, rows, offset):
    shape = (rows, TOK)
    pos = first_token + lax.broadcasted_iota(jnp.int32, shape, 1)
    row = lax.broadcasted_iota(jnp.int32, shape, 0) - offset
    video = jnp.zeros(shape, jnp.int32)
    end = 0
    for i in range(16):
        end = end + lengths_ref[i]
        video = video + jnp.where(pos >= end, 1, 0)
    both = row & video
    parity = (both ^ (both >> 1) ^ (both >> 2) ^ (video >> 3)) & 1
    return (1 - 2 * parity).astype(F32)


def kernel(
    lengths_ref, q_ref, k_ref, v_ref, w_ref, out_ref,
    kvs, qs, win, qw, kp, vp, qn, top, acc, wp, wr, ob, ao, ap, part, part_in,
    send, recv,
):
    seq, h = lax.axis_index("seq"), lax.axis_index("head")
    quads = lax.axis_size("seq") // QUAD
    g, j = seq // QUAD, seq % QUAD
    z, c = j // 2, j % 2
    left = ((g + quads - 1) % quads) * QUAD + j
    right = ((g + 1) % quads) * QUAD + j
    p1 = h + 1 - 2 * (h % 2)
    p2 = 3 - h

    def member(o):
        return 2 * ((z + o // 2) % 2) + (c + o % 2) % 2

    def copy(src, dst, s, r, seq_to, head_to):
        return pltpu.make_async_remote_copy(
            src_ref=src, dst_ref=dst, send_sem=send.at[s], recv_sem=recv.at[r],
            device_id=(seq_to, head_to), device_id_type=MESH,
        )

    barrier = pltpu.get_barrier_semaphore()

    def greet(seq_to, head_to):
        pl.semaphore_signal(barrier, inc=1, device_id=(seq_to, head_to), device_id_type=MESH)

    greet(left, h)
    greet(right, h)
    for o in range(QUAD):
        if o > 0:
            greet(g * QUAD + member(o), h)
        greet(g * QUAD + member(o), p1)
        greet(g * QUAD + member(o), p2)

    for i in range(QUAD):
        rows = slice(HEAD_DIM * i, HEAD_DIM * (i + 1))
        kvs[i] = jnp.concatenate([k_ref[rows, :], v_ref[rows, :]], axis=0)
    own_code = video_code(lengths_ref, seq * TOK, 8, 0).astype(BF16)
    for i in range(QUAD):
        rows = slice(HEAD_DIM * i, HEAD_DIM * (i + 1))
        qs[i] = jnp.concatenate([q_ref[rows, :], own_code], axis=0)
    pl.semaphore_wait(barrier, 13)

    def near(src, blk):
        for to, slot, way in ((right, 4, 0), (left, 12, 1)):
            copy(src, win.at[slot + blk], S_NEAR + 2 * blk + way, R_KV + slot + blk, to, h).start()

    for o in (2, 3, 1):
        i = member(o)
        copy(kvs.at[i], win.at[8 + j], S_KV + o, R_KV + 8 + j, g * QUAD + i, h).start()
        if o == 2:
            near(kvs.at[j], j)
    for o in (2, 3, 1):
        i = member(o)
        copy(qs.at[i], qw.at[j], S_Q + o, R_Q + j, g * QUAD + i, h).start()
    win[8 + j] = kvs[j]
    qw[j] = qs[j]

    cols = QUAD * HEAD_DIM
    r = lax.broadcasted_iota(jnp.int32, (cols, QUAD * PAD), 0)
    col = lax.broadcasted_iota(jnp.int32, (cols, QUAD * PAD), 1)
    from_row = HEAD_DIM * (col // PAD) + col % PAD - (PAD - HEAD_DIM)
    spread = jnp.where((col % PAD >= PAD - HEAD_DIM) & (r == from_row), 1.0, 0.0).astype(BF16)
    for b in range(4):
        wp[b] = lax.dot_general(
            w_ref[:, cols * b : cols * (b + 1)], spread, (((0,), (0,)), ((), ())), preferred_element_type=F32
        ).astype(BF16)
    to_pair = jnp.where(z == 1, (h + 1) % 4, (h + 3) % 4)
    pair_1 = to_pair + 1 - 2 * (to_pair % 2)
    beyond = jnp.where(pair_1 == h, 3 - to_pair, pair_1)
    piece = 2 * (1 - (h + z) % 2) + c
    copy(
        wp.at[jnp.where(c == 0, to_pair, beyond)], wr.at[piece], S_W, R_W + piece,
        g * QUAD + 2 * (1 - z) + c, to_pair,
    ).start()

    row16 = lax.broadcasted_iota(jnp.int32, (16, TOK), 0)

    def arrived(slot):
        copy(win.at[slot], win.at[slot], S_KV, R_KV + slot, seq, h).wait_recv()

    def augment(slot):
        blocks = quads * QUAD
        first = ((g * QUAD + slot - 8 + blocks) % blocks) * TOK
        code = (CODE * video_code(lengths_ref, first, 16, 8)).astype(BF16)
        middle = win[slot, 80:96, :]
        kp[slot, 0:80, :] = win[slot, 0:80, :]
        kp[slot, 80:96, :] = jnp.where(row16 < 8, middle, code)
        vp[slot, 0:16, :] = jnp.where(row16 < 8, jnp.ones_like(middle), middle)
        vp[slot, 16:96, :] = win[slot, 96:176, :]

    def queries_of(blk):
        qn[pl.ds(pl.multiple_of(blk * TOK, TOK), TOK), :] = qw[blk].T

    def attend(t, slots, opening=False):
        at = pl.ds(t * TILE if isinstance(t, int) else pl.multiple_of(t * TILE, TILE), TILE)
        q = qn[at, :]
        scores = [jnp.dot(q, kp[s], preferred_element_type=F32) for s in slots]
        newest = jnp.max(scores[0], axis=1, keepdims=True)
        for s in scores[1:]:
            newest = jnp.maximum(newest, jnp.max(s, axis=1, keepdims=True))
        total = None
        if not opening:
            before = top[at, :]
            newest = jnp.maximum(before, newest)
            total = acc[at, :] * jnp.exp2((before - newest) * EXPONENT)
        for s, slot in zip(scores, slots):
            weights = jnp.exp2((s - newest) * EXPONENT).astype(BF16)
            term = lax.dot_general(weights, vp[slot], (((1,), (1,)), ((), ())), preferred_element_type=F32)
            total = term if total is None else total + term
        top[at, :] = newest
        acc[at, :] = total

    def attend_block(blk, slots, opening=False):
        for half in range(2):
            attend(2 * blk + half, slots, opening)

    here, there = [j, member(1)], [member(2), member(3)]

    augment(8 + j)
    queries_of(j)
    arrived(8 + here[1])
    near(win.at[8 + here[1]], here[1])
    augment(8 + here[1])
    copy(qw.at[here[1]], qw.at[here[1]], S_Q, R_Q + here[1], seq, h).wait_recv()
    queries_of(here[1])
    for blk in here:
        attend_block(blk, [8 + i for i in here], opening=True)
    for blk in there:
        arrived(8 + blk)
        near(win.at[8 + blk], blk)
    for blk in there:
        augment(8 + blk)
    for blk in here:
        for first in (4, 12):
            arrived(first + blk)
            augment(first + blk)
    early = [first + i for first in (4, 12) for i in here]
    for blk in here:
        attend_block(blk, [8 + i for i in there] + early)
    for blk in there:
        copy(qw.at[blk], qw.at[blk], S_Q, R_Q + blk, seq, h).wait_recv()
        queries_of(blk)
    for blk in there:
        attend_block(blk, [8, 9, 10, 11] + early, opening=True)

    for blk in there:
        for first in (4, 12):
            arrived(first + blk)
    for n in range(QUAD):
        for to, src, slot, blk, way in ((right, 4, 0, 3 - n, 0), (left, 12, 16, n, 1)):
            copy(win.at[src + blk], win.at[slot + blk], S_FAR + 2 * blk + way, R_KV + slot + blk, to, h).start()
    copy(wr.at[piece], wr.at[piece], S_W, R_W + piece, seq, h).wait_recv()
    for o in range(1, QUAD):
        copy(wr.at[piece], wr.at[piece], S_WQ + o, R_W + piece, g * QUAD + member(o), h).start()
    for blk in there:
        for first in (4, 12):
            augment(first + blk)
    for blk in range(QUAD):
        attend_block(blk, [first + i for first in (4, 12) for i in there])

    def finish(b):
        for half, pair in ((0, p1), (1, p2)):
            at = slice((2 * b + half) * TILE, (2 * b + half + 1) * TILE)
            total = acc[at, :]
            ob[b, :, half * TILE : (half + 1) * TILE] = (total / total[:, 0:1]).T.astype(BF16)
        to = g * QUAD + b

        for half, pair in ((0, p1), (1, p2)):
            copy(
                ob.at[b, :, pl.ds(half * TILE, TILE)], ap.at[half, j],
                S_PAIR + 2 * b + half, R_PAIR + 4 * half + j, to, pair,
            ).start()

        @pl.when(j != b)
        def _():
            copy(ob.at[b], ao.at[j], S_OWN + b, R_OWN + j, to, h).start()

        @pl.when(j == b)
        def _():
            ao[j] = ob[b]

    def far_round(n, work):
        for slot in (3 - n, 16 + n):
            arrived(slot)
            augment(slot)
        for b, slots in work:
            attend_block(b, slots)

    far_round(0, [(b, [3, 16]) for b in range(4)])
    far_round(1, [(0, [2]), (1, [2, 17]), (2, [2, 17]), (3, [17])])
    far_round(2, [(1, [1]), (2, [18])])
    finish(1)
    finish(2)
    for b, slot in ((0, 1), (3, 18)):
        attend_block(b, [slot])
    far_round(3, [(0, [0]), (3, [19])])
    finish(0)
    finish(3)

    for o in range(1, QUAD):
        i = member(o)
        i = 2 * (1 - (h + i // 2) % 2) + i % 2
        copy(wr.at[i], wr.at[i], S_W, R_W + i, seq, h).wait_recv()
    for o in range(1, QUAD):
        blk = member(o)
        copy(ao.at[blk], ao.at[blk], S_OWN, R_OWN + blk, seq, h).wait_recv()
    sums = []
    for half, beyond in ((0, p2), (1, p1)):
        for blk in range(QUAD):
            copy(ap.at[half, blk], ap.at[half, blk], S_PAIR, R_PAIR + 4 * half + blk, seq, h).wait_recv()
        mine = ao[:, :, half * TILE : (half + 1) * TILE].reshape(QUAD * PAD, TILE)
        theirs = ap[half].reshape(QUAD * PAD, TILE)
        part[half] = (
            jnp.dot(wp[beyond], mine, preferred_element_type=F32)
            + jnp.dot(wr[2 * half + 1], theirs, preferred_element_type=F32)
        ).astype(BF16)
        copy(part.at[half], part_in.at[half], S_PART + half, R_PART + half, seq, beyond).start()
        sums.append(
            jnp.dot(wp[h], mine, preferred_element_type=F32)
            + jnp.dot(wr[2 * half], theirs, preferred_element_type=F32)
        )
    for half in range(2):
        copy(part_in.at[half], part_in.at[half], S_PART, R_PART + half, seq, h).wait_recv()
        out_ref[:, half * TILE : (half + 1) * TILE] = (sums[half] + part_in[half].astype(F32)).astype(BF16)

    for o in range(1, QUAD):
        copy(kvs.at[0], kvs.at[0], S_KV + o, R_KV, seq, h).wait_send()
        copy(qs.at[0], qs.at[0], S_Q + o, R_Q, seq, h).wait_send()
        copy(wr.at[0], wr.at[0], S_WQ + o, R_W, seq, h).wait_send()
    for n in range(16):
        copy(win.at[0], win.at[0], S_NEAR + n, R_KV, seq, h).wait_send()
    copy(wp.at[0], wp.at[0], S_W, R_W, seq, h).wait_send()
    for b in range(QUAD):

        @pl.when(j != b)
        def _():
            copy(ob.at[0], ob.at[0], S_OWN + b, R_OWN, seq, h).wait_send()

    for n in range(8):
        copy(ap.at[0, 0], ap.at[0, 0], S_PAIR + n, R_PAIR, seq, h).wait_send()
    for n in range(2):
        copy(part.at[0], part.at[0], S_PART + n, R_PART, seq, h).wait_send()


def body(queries, keys, values, lengths, out_weight):
    cols = QUAD * HEAD_DIM
    vmem = pl.BlockSpec(memory_space=pltpu.VMEM)
    out = pl.pallas_call(
        kernel,
        out_shape=jax.ShapeDtypeStruct((cols, TOK), BF16),
        in_specs=[pl.BlockSpec(memory_space=pltpu.SMEM)] + [vmem] * 4,
        out_specs=vmem,
        scratch_shapes=[
            pltpu.VMEM((QUAD, 2 * HEAD_DIM, TOK), BF16),
            pltpu.VMEM((QUAD, PAD, TOK), BF16),
            pltpu.VMEM((SLOTS, 2 * HEAD_DIM, TOK), BF16),
            pltpu.VMEM((QUAD, PAD, TOK), BF16),
            pltpu.VMEM((SLOTS, PAD, TOK), BF16),
            pltpu.VMEM((SLOTS, PAD, TOK), BF16),
            pltpu.VMEM((QUAD * TOK, PAD), BF16),
            pltpu.VMEM((QUAD * TOK, 1), F32),
            pltpu.VMEM((QUAD * TOK, PAD), F32),
            pltpu.VMEM((4, cols, QUAD * PAD), BF16),
            pltpu.VMEM((4, cols, QUAD * PAD), BF16),
            pltpu.VMEM((QUAD, PAD, TOK), BF16),
            pltpu.VMEM((QUAD, PAD, TOK), BF16),
            pltpu.VMEM((2, QUAD, PAD, TILE), BF16),
            pltpu.VMEM((2, cols, TILE), BF16),
            pltpu.VMEM((2, cols, TILE), BF16),
            pltpu.SemaphoreType.DMA((S_END,)),
            pltpu.SemaphoreType.DMA((R_END,)),
        ],
        compiler_params=pltpu.CompilerParams(
            collective_id=0, has_side_effects=True, vmem_limit_bytes=56 << 20
        ),
    )(lengths, queries.T, keys.T, values.T, out_weight)
    return out.T


def solution(mesh):
    in_specs = (P("seq", "head"), P("seq", "head"), P("seq", "head"), P(), P("head", None))
    out_specs = P("seq", "head")
    return jax.shard_map(body, mesh=mesh, in_specs=in_specs, out_specs=out_specs, check_vma=False)
```

```python
import functools

import jax
import jax.numpy as jnp
from jax import lax
from jax.experimental import pallas as pl
from jax.experimental.pallas import tpu as pltpu
from jax.sharding import PartitionSpec as P

HEAD_DIM = 88
PAD = 96
TOK = 512
QUAD = 4
TILE = 256
SLOTS = 20
EXPONENT = 1.4426950408889634 / HEAD_DIM**0.5
CODE = 1536.0
MESH = pl.DeviceIdType.MESH
F32 = jnp.float32
BF16 = jnp.bfloat16

S_KV, S_Q, S_NEAR, S_FAR, S_W, S_WQ, S_OWN, S_PAIR, S_PART, S_END = 0, 4, 8, 16, 24, 25, 29, 33, 41, 43
R_KV, R_Q, R_W, R_OWN, R_PAIR, R_PART, R_END = 0, 20, 24, 28, 32, 40, 42


def video_code(lengths_ref, first_token, rows, offset):
    shape = (rows, TOK)
    pos = first_token + lax.broadcasted_iota(jnp.int32, shape, 1)
    row = lax.broadcasted_iota(jnp.int32, shape, 0) - offset
    video = jnp.zeros(shape, jnp.int32)
    end = 0
    for i in range(16):
        end = end + lengths_ref[i]
        video = video + jnp.where(pos >= end, 1, 0)
    both = row & video
    parity = (both ^ (both >> 1) ^ (both >> 2) ^ (video >> 3)) & 1
    return (1 - 2 * parity).astype(F32)


def kernel(
    lengths_ref, q_ref, k_ref, v_ref, w_ref, out_ref,
    kvs, qs, win, qw, kp, vp, qn, top, acc, wp, wr, ob, ao, ap, part, part_in,
    send, recv,
):
    seq, h = lax.axis_index("seq"), lax.axis_index("head")
    quads = lax.axis_size("seq") // QUAD
    g, j = seq // QUAD, seq % QUAD
    z, c = j // 2, j % 2
    left = ((g + quads - 1) % quads) * QUAD + j
    right = ((g + 1) % quads) * QUAD + j
    p1 = h + 1 - 2 * (h % 2)
    p2 = 3 - h

    def member(o):
        return 2 * ((z + o // 2) % 2) + (c + o % 2) % 2

    def copy(src, dst, s, r, seq_to, head_to):
        return pltpu.make_async_remote_copy(
            src_ref=src, dst_ref=dst, send_sem=send.at[s], recv_sem=recv.at[r],
            device_id=(seq_to, head_to), device_id_type=MESH,
        )

    barrier = pltpu.get_barrier_semaphore()

    def greet(seq_to, head_to):
        pl.semaphore_signal(barrier, inc=1, device_id=(seq_to, head_to), device_id_type=MESH)

    greet(left, h)
    greet(right, h)
    for o in range(QUAD):
        if o > 0:
            greet(g * QUAD + member(o), h)
        greet(g * QUAD + member(o), p1)
        greet(g * QUAD + member(o), p2)

    for i in range(QUAD):
        rows = slice(HEAD_DIM * i, HEAD_DIM * (i + 1))
        kvs[i] = jnp.concatenate([k_ref[rows, :], v_ref[rows, :]], axis=0)
    own_code = video_code(lengths_ref, seq * TOK, 8, 0).astype(BF16)
    for i in range(QUAD):
        rows = slice(HEAD_DIM * i, HEAD_DIM * (i + 1))
        qs[i] = jnp.concatenate([q_ref[rows, :], own_code], axis=0)
    pl.semaphore_wait(barrier, 13)

    def near(src, blk):
        for to, slot, way in ((right, 4, 0), (left, 12, 1)):
            copy(src, win.at[slot + blk], S_NEAR + 2 * blk + way, R_KV + slot + blk, to, h).start()

    for o in (2, 3, 1):
        i = member(o)
        copy(kvs.at[i], win.at[8 + j], S_KV + o, R_KV + 8 + j, g * QUAD + i, h).start()
        if o == 2:
            near(kvs.at[j], j)
    for o in (2, 3, 1):
        i = member(o)
        copy(qs.at[i], qw.at[j], S_Q + o, R_Q + j, g * QUAD + i, h).start()
    win[8 + j] = kvs[j]
    qw[j] = qs[j]

    cols = QUAD * HEAD_DIM
    r = lax.broadcasted_iota(jnp.int32, (cols, QUAD * PAD), 0)
    col = lax.broadcasted_iota(jnp.int32, (cols, QUAD * PAD), 1)
    from_row = HEAD_DIM * (col // PAD) + col % PAD - (PAD - HEAD_DIM)
    spread = jnp.where((col % PAD >= PAD - HEAD_DIM) & (r == from_row), 1.0, 0.0).astype(BF16)
    for b in range(4):
        wp[b] = lax.dot_general(
            w_ref[:, cols * b : cols * (b + 1)], spread, (((0,), (0,)), ((), ())), preferred_element_type=F32
        ).astype(BF16)
    to_pair = jnp.where(z == 1, (h + 1) % 4, (h + 3) % 4)
    pair_1 = to_pair + 1 - 2 * (to_pair % 2)
    beyond = jnp.where(pair_1 == h, 3 - to_pair, pair_1)
    piece = 2 * (1 - (h + z) % 2) + c

    copy(
        wp.at[jnp.where(c == 0, to_pair, beyond)], wr.at[piece], S_W, R_W + piece,
        g * QUAD + 2 * (1 - z) + c, to_pair,
    ).start()

    row16 = lax.broadcasted_iota(jnp.int32, (16, TOK), 0)

    def arrived(slot):
        copy(win.at[slot], win.at[slot], S_KV, R_KV + slot, seq, h).wait_recv()

    def augment(slot):
        blocks = quads * QUAD
        first = ((g * QUAD + slot - 8 + blocks) % blocks) * TOK
        code = (CODE * video_code(lengths_ref, first, 16, 8)).astype(BF16)
        middle = win[slot, 80:96, :]
        kp[slot, 0:80, :] = win[slot, 0:80, :]
        kp[slot, 80:96, :] = jnp.where(row16 < 8, middle, code)
        vp[slot, 0:16, :] = jnp.where(row16 < 8, jnp.ones_like(middle), middle)
        vp[slot, 16:96, :] = win[slot, 96:176, :]

    def queries_of(blk):
        qn[pl.ds(pl.multiple_of(blk * TOK, TOK), TOK), :] = qw[blk].T

    def attend(work, opening=False):
        tiles = []
        for blk, slots in work:
            for half in range(2):
                parts = []
                for slot in slots:
                    inner = isinstance(blk, int) and isinstance(slot, int)
                    lo = TILE if inner and half == 1 and slot == blk else 0
                    hi = TILE if inner and half == 0 and slot == blk + 16 else TOK
                    parts.append((slot, lo, hi))
                t = 2 * blk + half
                at = pl.ds(t * TILE if isinstance(t, int) else pl.multiple_of(t * TILE, TILE), TILE)
                before = (None, None) if opening else (top[at, :], acc[at, :])
                tiles.append((at, qn[at, :], *before, parts))
        results = []
        for at, q, before, total, parts in tiles:
            scores = [jnp.dot(q, kp[s, :, lo:hi], preferred_element_type=F32) for s, lo, hi in parts]
            newest = before
            for s in scores:
                most = jnp.max(s, axis=1, keepdims=True)
                newest = most if newest is None else jnp.maximum(newest, most)
            if not opening:
                total = total * jnp.exp2((before - newest) * EXPONENT)
            for s, (slot, lo, hi) in zip(scores, parts):
                weights = jnp.exp2((s - newest) * EXPONENT).astype(BF16)
                term = lax.dot_general(
                    weights, vp[slot, :, lo:hi], (((1,), (1,)), ((), ())), preferred_element_type=F32
                )
                total = term if total is None else total + term
            results.append((at, newest, total))
        for at, newest, total in results:
            top[at, :] = newest
            acc[at, :] = total

    here, there = [j, member(1)], [member(2), member(3)]

    augment(8 + j)
    queries_of(j)
    arrived(8 + here[1])
    near(win.at[8 + here[1]], here[1])
    augment(8 + here[1])
    copy(qw.at[here[1]], qw.at[here[1]], S_Q, R_Q + here[1], seq, h).wait_recv()
    queries_of(here[1])
    attend([(blk, [8 + i for i in here]) for blk in here], opening=True)
    for blk in there:
        arrived(8 + blk)
        near(win.at[8 + blk], blk)
    for blk in there:
        augment(8 + blk)
    attend([(blk, [8 + i for i in there]) for blk in here])
    for blk in there:
        copy(qw.at[blk], qw.at[blk], S_Q, R_Q + blk, seq, h).wait_recv()
        queries_of(blk)
    attend([(blk, [8, 9, 10, 11]) for blk in there], opening=True)
    copy(wr.at[piece], wr.at[piece], S_W, R_W + piece, seq, h).wait_recv()
    for o in range(1, QUAD):
        copy(wr.at[piece], wr.at[piece], S_WQ + o, R_W + piece, g * QUAD + member(o), h).start()
    for blk in here:
        for first in (4, 12):
            arrived(first + blk)
            augment(first + blk)
    early = [first + i for first in (4, 12) for i in here]
    attend([(blk, early) for blk in range(3)])
    for blk in there:
        for first in (4, 12):
            arrived(first + blk)

    for n in range(QUAD):
        for to, src, slot, blk, way in ((right, 4, 0, 3 - n, 0), (left, 12, 16, n, 1)):
            copy(win.at[src + blk], win.at[slot + blk], S_FAR + 2 * blk + way, R_KV + slot + blk, to, h).start()

    attend([(3, early)])
    for blk in there:
        for first in (4, 12):
            augment(first + blk)
    attend([(blk, [first + i for first in (4, 12) for i in there]) for blk in range(QUAD)])

    def finish(b):
        for half, pair in ((0, p1), (1, p2)):
            at = slice((2 * b + half) * TILE, (2 * b + half + 1) * TILE)
            total = acc[at, :]
            ob[b, :, half * TILE : (half + 1) * TILE] = (total / total[:, 0:1]).astype(BF16).T
        to = g * QUAD + b

        for half, pair in ((0, p1), (1, p2)):
            copy(
                ob.at[b, :, pl.ds(half * TILE, TILE)], ap.at[half, j],
                S_PAIR + 2 * b + half, R_PAIR + 4 * half + j, to, pair,
            ).start()

        @pl.when(j != b)
        def _():
            copy(ob.at[b], ao.at[j], S_OWN + b, R_OWN + j, to, h).start()

        @pl.when(j == b)
        def _():
            ao[j] = ob[b]

    def far_round(n, work):
        for slot in (3 - n, 16 + n):
            arrived(slot)
            augment(slot)
        attend(work)

    far_round(0, [(b, [3, 16]) for b in range(4)])
    far_round(1, [(0, [2]), (1, [2, 17]), (2, [2, 17]), (3, [17])])
    far_round(2, [(1, [1]), (2, [18])])
    finish(1)
    finish(2)
    attend([(0, [1]), (3, [18])])
    far_round(3, [(0, [0]), (3, [19])])
    finish(0)
    finish(3)

    for o in range(1, QUAD):
        i = member(o)
        i = 2 * (1 - (h + i // 2) % 2) + i % 2
        copy(wr.at[i], wr.at[i], S_W, R_W + i, seq, h).wait_recv()
    for o in range(1, QUAD):
        blk = member(o)
        copy(ao.at[blk], ao.at[blk], S_OWN, R_OWN + blk, seq, h).wait_recv()
    sums = []
    for half, beyond in ((0, p2), (1, p1)):
        for blk in range(QUAD):
            copy(ap.at[half, blk], ap.at[half, blk], S_PAIR, R_PAIR + 4 * half + blk, seq, h).wait_recv()
        mine = ao[:, :, half * TILE : (half + 1) * TILE].reshape(QUAD * PAD, TILE)
        theirs = ap[half].reshape(QUAD * PAD, TILE)
        part[half] = (
            jnp.dot(wp[beyond], mine, preferred_element_type=F32)
            + jnp.dot(wr[2 * half + 1], theirs, preferred_element_type=F32)
        ).astype(BF16)
        copy(part.at[half], part_in.at[half], S_PART + half, R_PART + half, seq, beyond).start()
        sums.append(
            jnp.dot(wp[h], mine, preferred_element_type=F32)
            + jnp.dot(wr[2 * half], theirs, preferred_element_type=F32)
        )
    for half in range(2):
        copy(part_in.at[half], part_in.at[half], S_PART, R_PART + half, seq, h).wait_recv()
        out_ref[:, half * TILE : (half + 1) * TILE] = (sums[half] + part_in[half].astype(F32)).astype(BF16)

    for o in range(1, QUAD):
        copy(kvs.at[0], kvs.at[0], S_KV + o, R_KV, seq, h).wait_send()
        copy(qs.at[0], qs.at[0], S_Q + o, R_Q, seq, h).wait_send()
        copy(wr.at[0], wr.at[0], S_WQ + o, R_W, seq, h).wait_send()
    for n in range(16):
        copy(win.at[0], win.at[0], S_NEAR + n, R_KV, seq, h).wait_send()
    copy(wp.at[0], wp.at[0], S_W, R_W, seq, h).wait_send()
    for b in range(QUAD):

        @pl.when(j != b)
        def _():
            copy(ob.at[0], ob.at[0], S_OWN + b, R_OWN, seq, h).wait_send()

    for n in range(8):
        copy(ap.at[0, 0], ap.at[0, 0], S_PAIR + n, R_PAIR, seq, h).wait_send()
    for n in range(2):
        copy(part.at[0], part.at[0], S_PART + n, R_PART, seq, h).wait_send()


def body(queries, keys, values, lengths, out_weight):
    cols = QUAD * HEAD_DIM
    vmem = pl.BlockSpec(memory_space=pltpu.VMEM)
    out = pl.pallas_call(
        kernel,
        out_shape=jax.ShapeDtypeStruct((cols, TOK), BF16),
        in_specs=[pl.BlockSpec(memory_space=pltpu.SMEM)] + [vmem] * 4,
        out_specs=vmem,
        scratch_shapes=[
            pltpu.VMEM((QUAD, 2 * HEAD_DIM, TOK), BF16),
            pltpu.VMEM((QUAD, PAD, TOK), BF16),
            pltpu.VMEM((SLOTS, 2 * HEAD_DIM, TOK), BF16),
            pltpu.VMEM((QUAD, PAD, TOK), BF16),
            pltpu.VMEM((SLOTS, PAD, TOK), BF16),
            pltpu.VMEM((SLOTS, PAD, TOK), BF16),
            pltpu.VMEM((QUAD * TOK, PAD), BF16),
            pltpu.VMEM((QUAD * TOK, 1), F32),
            pltpu.VMEM((QUAD * TOK, PAD), F32),
            pltpu.VMEM((4, cols, QUAD * PAD), BF16),
            pltpu.VMEM((4, cols, QUAD * PAD), BF16),
            pltpu.VMEM((QUAD, PAD, TOK), BF16),
            pltpu.VMEM((QUAD, PAD, TOK), BF16),
            pltpu.VMEM((2, QUAD, PAD, TILE), BF16),
            pltpu.VMEM((2, cols, TILE), BF16),
            pltpu.VMEM((2, cols, TILE), BF16),
            pltpu.SemaphoreType.DMA((S_END,)),
            pltpu.SemaphoreType.DMA((R_END,)),
        ],
        compiler_params=pltpu.CompilerParams(
            collective_id=0, has_side_effects=True, vmem_limit_bytes=56 << 20
        ),
    )(lengths, queries.T, keys.T, values.T, out_weight)
    return out.T


def solution(mesh):
    in_specs = (P("seq", "head"), P("seq", "head"), P("seq", "head"), P(), P("head", None))
    out_specs = P("seq", "head")
    return jax.shard_map(body, mesh=mesh, in_specs=in_specs, out_specs=out_specs, check_vma=False)
```
